32 devices in a mesh: chain: 2 (over x), row: 16 (over z, y, core).
Axes of the slice: x: 2, y: 2, z: 4, core: 2. Of those that a mesh axis runs over, the one named last changes fastest.
Arguments:
- neighbours: int32 [128, 36], P(('chain', 'row')), parts along dimension 0, may hold values from -1 to 63, as said below
- coordinates: float32 [2, 65536], P(None, ('chain', 'row')), parts along dimension 1, may hold values from 0 to 8, as said below
- right_side: float32 [65536], P(('chain', 'row')), parts along dimension 0, may hold values from -9 to 9
Outputs:
- solution_field: float32 [65536], P(('chain', 'row')), parts along dimension 0
- residual: float32 [65536], P(('chain', 'row')), parts along dimension 0
The draws below stay inside these ranges and needn't reach their ends.
There are 2 independent parts, one for each index of `chain`. The reference program is written for one: setup_inputs(seed, part) draws one part's arguments, and reference() takes and returns one part's arrays. A program takes and returns all parts, laid end to end along the dimension named above; each array names one. Nothing has to cross between parts.
Inputs may be any that keep to these rules, and one draw needn't show every extreme that they name: `neighbours`: every lattice cell holds 1 to 4 tiles and some cell holds 4. Row t lists, in increasing order and before all -1 entries, exactly the tiles whose cell is tile t's cell or one of the eight cells around it; the lists are symmetric and each contains t. `coordinates`: the points of tile t lie in one unit cell [i, i + 1) x [j, j + 1) of a lattice of 4 x 8 cells, the cell of that tile.
All inputs are finite; a program needn't handle non-finite values.
Results may differ from the reference program's by a relative error of at most 0.0003.
Values sent between devices are 32-bit elements; how exact they have to be, the bound alone decides.
A program may use at most 64 MiB of HBM per device.

```python
import jax
import jax.numpy as jnp
from jax import lax

TILE = 512
MOST = 4
ITERS = 3
NBR = 36
TILES = 64
POINTS = 32768
CELLS = 32
CELLS_Y = 8


def layout_cells(key):
    slots = CELLS * MOST
    key_full, key_score, key_mix = jax.random.split(key, 3)
    full_cell = jax.random.randint(key_full, (), 0, CELLS)
    scores = jax.random.permutation(key_score, slots).astype(jnp.int32)
    slot_ids = jnp.arange(slots, dtype=jnp.int32)
    forced = (slot_ids % MOST == 0) | (slot_ids // MOST == full_cell)
    scores = jnp.where(forced, scores - slots, scores)
    ranked = jnp.argsort(scores, stable=True).astype(jnp.int32)
    chosen = ranked[:TILES]
    mixing = jax.random.permutation(key_mix, TILES).astype(jnp.int32)
    return (chosen[mixing] // MOST).astype(jnp.int32)


def draw_neighbours(key, part):
    cells = layout_cells(key)
    cell_x = cells // CELLS_Y
    cell_y = cells % CELLS_Y
    close = (jnp.abs(cell_x[:, None] - cell_x[None, :]) <= 1) & (jnp.abs(cell_y[:, None] - cell_y[None, :]) <= 1)
    tile_ids = jnp.arange(TILES, dtype=jnp.int32)
    keyed = jnp.where(close, tile_ids[None, :], TILES + tile_ids[None, :])
    filler = jnp.full((TILES, NBR), 2 * TILES, jnp.int32)
    ordered = jnp.sort(jnp.concatenate([keyed, filler], axis=1), axis=1)[:, :NBR]
    return jnp.where(ordered < TILES, ordered, -1).astype(jnp.int32)


def draw_coordinates(key, part):
    cells = layout_cells(key)
    key = jax.random.fold_in(key, 7)
    inside = jax.random.uniform(key, (2, TILES, TILE), jnp.float32, 0.0, 0.999)
    corner = jnp.stack([(cells // CELLS_Y).astype(jnp.float32), (cells % CELLS_Y).astype(jnp.float32)])
    return (corner[:, :, None] + inside).reshape(2, POINTS)


def draw_right_side(key, part):
    key = jax.random.fold_in(key, 9)
    place = jnp.arange(POINTS, dtype=jnp.float32) / POINTS
    values = jnp.clip(jax.random.normal(key, (POINTS,), jnp.float32), -4.0, 4.0)
    return 0.6 * values * jnp.power(3.0, place)


def setup_inputs(seed: int = 0, part: int = 0) -> dict:
    arg_keys = jax.random.split(jax.random.key(seed), 4)
    own_keys = jax.random.split(jax.random.fold_in(arg_keys[3], part), 4)
    return {
        "neighbours": draw_neighbours(jax.random.fold_in(jax.random.fold_in(arg_keys[3], part), 71), part),
        "coordinates": draw_coordinates(jax.random.fold_in(jax.random.fold_in(arg_keys[3], part), 71), part),
        "right_side": draw_right_side(jax.random.fold_in(jax.random.fold_in(arg_keys[3], part), 71), part),
    }


nugget = 1.0
kernel_scale = 10.0

def kernel_tile(row_points, col_points):
    delta_x = row_points[0][:, None] - col_points[0][None, :]
    delta_y = row_points[1][:, None] - col_points[1][None, :]
    radius = jnp.sqrt(delta_x * delta_x + delta_y * delta_y)
    shrink = jnp.maximum(1.0 - radius, 0.0)
    return shrink * shrink * (shrink * shrink) * (4.0 * radius + 1.0)

def operate(values, coordinates, neighbours):
    points = coordinates.reshape(2, TILES, TILE)
    pieces = values.reshape(TILES, TILE)
    listed = lax.optimization_barrier(jnp.sum((neighbours >= 0).astype(jnp.int32), axis=1))

    def one_row(row_tile):

        def advance(position, summed):
            col_tile = neighbours[row_tile, position]
            weights = kernel_tile(points[:, row_tile], points[:, col_tile])
            return summed + jnp.dot(weights, pieces[col_tile], precision=lax.Precision.HIGHEST)
        return lax.fori_loop(0, listed[row_tile], advance, jnp.zeros((TILE,), jnp.float32))
    images = lax.map(one_row, jnp.arange(TILES, dtype=jnp.int32))
    return (nugget * pieces + kernel_scale / TILE * images).reshape(-1)

def reference(neighbours, coordinates, right_side):
    solution_field = jnp.zeros_like(right_side)
    residual = right_side
    direction = right_side
    norm_now = jnp.sum(residual * residual)
    for sweep in range(ITERS):
        image = operate(direction, coordinates, neighbours)
        alpha = norm_now / jnp.sum(direction * image)
        solution_field = solution_field + alpha * direction
        residual = residual - alpha * image
        norm_next = jnp.sum(residual * residual)
        direction = residual + norm_next / norm_now * direction
        norm_now = norm_next
    return (solution_field, residual)
```

```python
import jax
import jax.numpy as jnp
from jax import lax
from jax.experimental import pallas as pl
from jax.experimental.pallas import tpu as pltpu
from jax.sharding import PartitionSpec as P

ITERS = 3
DEPTH = 32

nugget = 1.0
kernel_scale = 10.0


def split(values):
    high = lax.reduce_precision(values, 8, 7)
    rest = values - high
    middle = lax.reduce_precision(rest, 8, 7)
    return high, middle, rest - middle


def features(x, y):
    left, right = [], []
    for part in (x, y):
        h, m, l = split(part)
        left += [-2.0 * h, -2.0 * h, -2.0 * m, -2.0 * m, -2.0 * h, -2.0 * l]
        right += [h, m, h, m, l, h]
    norm = split(x * x + y * y)
    one = jnp.ones_like(x)
    left += list(norm) + [one] * 3
    right += [one] * 3 + list(norm)
    zero = [jnp.zeros_like(x)] * (DEPTH - len(left))
    left = jnp.stack(left + zero, axis=1).astype(jnp.bfloat16)
    right = jnp.stack(right + zero, axis=1).astype(jnp.bfloat16)
    return left, right


def operate_kernel(counts, neighbours, left, right, values, image, summed):
    tiles_here, size, _ = left.shape
    rows = 128

    def one_row(t, carry):
        summed[...] = jnp.zeros_like(summed)

        def advance(position, carry):
            u = neighbours[t, position]
            v = values[pl.ds(u, 1), :]
            columns = right[u]
            for c in range(size // rows):
                here = pl.ds(c * rows, rows)
                square = jnp.dot(left[t, here, :], columns, preferred_element_type=jnp.float32)
                square = jnp.maximum(square, 1e-20)
                shrink = jnp.maximum(1.0 - square * lax.rsqrt(square), 0.0)
                fourth = shrink * shrink
                fourth = fourth * fourth
                term = fourth * (1.25 - shrink) * v
                total = term[:, :128]
                for k in range(1, size // 128):
                    total = total + term[:, k * 128 : (k + 1) * 128]
                summed[here, :] += total
            return carry

        lax.fori_loop(0, counts[t], advance, 0)
        image[pl.ds(t, 1), :] = jnp.sum(summed[...].T, axis=0, keepdims=True)
        return carry

    lax.fori_loop(0, tiles_here, one_row, 0)


def operate(counts, neighbours, left, right, values):
    tiles_here, size, _ = left.shape
    smem = pl.BlockSpec(memory_space=pltpu.SMEM)
    vmem = pl.BlockSpec(memory_space=pltpu.VMEM)
    return pl.pallas_call(
        operate_kernel,
        out_shape=jax.ShapeDtypeStruct((tiles_here, size), jnp.float32),
        in_specs=[smem, smem, vmem, vmem, vmem],
        out_specs=vmem,
        scratch_shapes=[pltpu.VMEM((size, 128), jnp.float32)],
        compiler_params=pltpu.CompilerParams(vmem_limit_bytes=40 * 1024 * 1024),
    )(counts, neighbours, left, right, values)


def on_device(neighbours, coordinates, right_side):
    tiles_here = neighbours.shape[0]
    size = right_side.shape[0] // tiles_here
    packed = jnp.concatenate([coordinates, right_side[None]], axis=0)
    every = lax.all_gather(packed, "row", axis=1, tiled=True).reshape(3, -1, size)
    total = every.shape[1]
    first = lax.axis_index("row") * tiles_here

    def mine(values):
        return lax.dynamic_slice_in_dim(values, first, tiles_here, 0)

    x, y = every[0] - 4.0, every[1] - 4.0
    left, right = features(x, y)
    left = jnp.swapaxes(mine(left), 1, 2)
    counts = jnp.sum((neighbours >= 0).astype(jnp.int32), axis=1)
    residual = direction = every[2]
    norm_now = jnp.sum(residual * residual)
    field = jnp.zeros((tiles_here, size), jnp.float32)
    for sweep in range(ITERS):
        part = operate(counts, neighbours, left, right, direction)
        own = mine(direction)
        part = nugget * own + (4.0 * kernel_scale / size) * part
        if sweep == ITERS - 1:
            alpha = norm_now / lax.psum(jnp.sum(own * part), "row")
            return (field + alpha * own).reshape(-1), (mine(residual) - alpha * part).reshape(-1)
        image = lax.all_gather(part, "row", axis=0, tiled=True)
        alpha = norm_now / jnp.sum(direction * image)
        field = field + alpha * own
        residual = residual - alpha * image
        norm_next = jnp.sum(residual * residual)
        direction = residual + norm_next / norm_now * direction
        norm_now = norm_next


def solution(mesh):
    return jax.shard_map(
        on_device,
        mesh=mesh,
        in_specs=(P(("chain", "row"), None), P(None, ("chain", "row")), P(("chain", "row"))),
        out_specs=(P(("chain", "row")), P(("chain", "row"))),
        check_vma=False,
    )
```

```python
import functools

import jax
import jax.numpy as jnp
from jax import lax
from jax.experimental import pallas as pl
from jax.experimental.pallas import tpu as pltpu
from jax.sharding import PartitionSpec as P

ITERS = 3
DEPTH = 32
MESH = pl.DeviceIdType.MESH

nugget = 1.0
kernel_scale = 10.0

VMEM = pl.BlockSpec(memory_space=pltpu.VMEM)
SMEM = pl.BlockSpec(memory_space=pltpu.SMEM)


def exchange(n, block, landed, send, recv):
    me = lax.axis_index("row")
    barrier = pltpu.get_barrier_semaphore()

    def greet(i, carry):
        pl.semaphore_signal(barrier, inc=1, device_id={"row": lax.rem(me + i, n)}, device_id_type=MESH)
        return carry

    lax.fori_loop(1, n, greet, 0)
    pl.semaphore_wait(barrier, n - 1)

    def copy(i, place):
        return pltpu.make_async_remote_copy(
            src_ref=block,
            dst_ref=landed.at[place],
            send_sem=send.at[i],
            recv_sem=recv.at[i],
            device_id={"row": lax.rem(me + i, n)},
            device_id_type=MESH,
        )

    def begin(i, carry):
        copy(i, me).start()
        return carry

    def end(i, carry):
        copy(i, me).wait_send()
        copy(i, lax.rem(me - i + n, n)).wait_recv()
        return carry

    lax.fori_loop(1, n, begin, 0)
    landed[me] = block[...]
    lax.fori_loop(1, n, end, 0)


def total(values):
    values = values[0] if values.shape[0] == 1 else jnp.sum(values, axis=0)
    return jnp.sum(values, keepdims=True)


def gather_kernel(n, block, every, landed, send, recv):
    exchange(n, block, landed, send, recv)
    every[...] = landed[...]


def update_kernel(n, scale, block, direction, residual, field, next_direction, next_residual, next_field, landed, send, recv):
    exchange(n, block, landed, send, recv)
    old, rest = direction[...], residual[...]
    image = nugget * old + scale * landed[...]
    norm_now = total(rest * rest)
    alpha = norm_now / total(old * image)
    next_field[...] = field[...] + alpha[None] * old
    rest = rest - alpha[None] * image
    next_residual[...] = rest
    next_direction[...] = rest + (total(rest * rest) / norm_now)[None] * old


def finish_kernel(n, scale, part, direction, residual, field, own_field, own_residual, block, landed, send, recv):
    me = lax.axis_index("row")
    own = direction[me]
    image = nugget * own + scale * part[...]
    block[...] = jnp.broadcast_to(jnp.sum(own * image, keepdims=True), block.shape)
    exchange(n, block, landed, send, recv)
    rest = residual[...]
    alpha = total(rest * rest) / jnp.sum(landed[...], axis=0)[:1, :1]
    own_field[...] = field[me] + alpha * own
    own_residual[...] = residual[me] - alpha * image


def talk(kernel, n, ident, block, outs, extra=()):
    return functools.partial(
        pl.pallas_call,
        kernel,
        out_shape=outs,
        scratch_shapes=[
            *extra,
            pltpu.VMEM((n, *block), jnp.float32),
            pltpu.SemaphoreType.DMA((n,)),
            pltpu.SemaphoreType.DMA((n,)),
        ],
        compiler_params=pltpu.CompilerParams(
            collective_id=ident, has_side_effects=True, vmem_limit_bytes=40 * 1024 * 1024
        ),
    )


def split(values):
    def rounded(part):
        return part.astype(jnp.bfloat16).astype(jnp.float32)

    high = rounded(values)
    rest = values - high
    middle = rounded(rest)
    return high, middle, rest - middle


def features_kernel(every, own, left, right):
    n, _, tiles_here, size = every.shape
    left[...] = jnp.zeros_like(left)
    right[...] = jnp.zeros_like(right)
    one = jnp.ones((1, size), jnp.float32)

    def centred(values):
        return [jnp.concatenate([values[c, pl.ds(t, 1), :] for c in range(2)], axis=0) - 4.0 for t in range(tiles_here)]

    def parts(point):
        norm = jnp.sum(point * point, axis=0, keepdims=True)
        return split(point), split(norm)

    def write(device, carry):
        for t, point in enumerate(centred(every.at[device])):
            (h, m, l), norm = parts(point)
            tile = device * tiles_here + t
            for k, rows in enumerate((h, m, h, m, l, h)):
                right[tile, 2 * k : 2 * k + 2, :] = rows
            for k in range(3):
                right[tile, 12 + k : 13 + k, :] = one
                right[tile, 15 + k : 16 + k, :] = norm[k]
        return carry

    lax.fori_loop(0, n, write, 0)
    for t, point in enumerate(centred(own)):
        (h, m, l), norm = parts(point)
        for k, rows in enumerate((h, h, m, m, h, l)):
            left[t, 2 * k : 2 * k + 2, :] = -2.0 * rows
        for k in range(3):
            left[t, 12 + k : 13 + k, :] = norm[k]
            left[t, 15 + k : 16 + k, :] = one


def operate_kernel(counts, neighbours, left, right, values, image, summed, turned):
    tiles_here, _, size = left.shape
    rows = 128

    def one_row(t, carry):
        summed[...] = jnp.zeros_like(summed)
        turned[...] = left[t].T.astype(jnp.bfloat16)

        def advance(position, carry):
            u = neighbours[t, position]
            v = values[u // tiles_here, pl.ds(u % tiles_here, 1), :]
            columns = right[u].astype(jnp.bfloat16)
            for c in range(size // rows):
                here = pl.ds(c * rows, rows)
                square = jnp.dot(turned[here, :], columns, preferred_element_type=jnp.float32)
                square = jnp.maximum(square, 1e-20)
                shrink = jnp.maximum(1.0 - square * lax.rsqrt(square), 0.0)
                fourth = shrink * shrink
                fourth = fourth * fourth
                term = fourth * (1.25 - shrink) * v
                added = term[:, :128]
                for k in range(1, size // 128):
                    added = added + term[:, k * 128 : (k + 1) * 128]
                summed[here, :] += added
            return carry

        lax.fori_loop(0, counts[t], advance, 0)
        image[pl.ds(t, 1), :] = jnp.sum(summed[...].T, axis=0, keepdims=True)
        return carry

    lax.fori_loop(0, tiles_here, one_row, 0)


def on_device(neighbours, coordinates, right_side):
    n = lax.axis_size("row")
    tiles_here = neighbours.shape[0]
    size = right_side.shape[0] // tiles_here
    tile_count = n * tiles_here
    scale = 4.0 * kernel_scale / size
    f32 = lambda *shape: jax.ShapeDtypeStruct(shape, jnp.float32)
    whole, own = f32(n, tiles_here, size), f32(tiles_here, size)
    limit = pltpu.CompilerParams(vmem_limit_bytes=48 * 1024 * 1024)

    points = coordinates.reshape(2, tiles_here, size)
    packed = jnp.concatenate([points, right_side.reshape(1, tiles_here, size)], axis=0)
    block = (3, tiles_here, size)
    every = talk(functools.partial(gather_kernel, n), n, 0, block, f32(n, *block))(in_specs=[VMEM], out_specs=VMEM)(packed)
    left, right = pl.pallas_call(
        features_kernel,
        out_shape=(f32(tiles_here, DEPTH, size), f32(tile_count, DEPTH, size)),
        in_specs=[VMEM] * 2,
        out_specs=(VMEM, VMEM),
        compiler_params=limit,
    )(every, points)
    counts = jnp.sum((neighbours >= 0).astype(jnp.int32), axis=1)
    residual = direction = every[:, 2]
    field = jnp.zeros(whole.shape, jnp.float32)
    for sweep in range(ITERS):
        part = pl.pallas_call(
            operate_kernel,
            out_shape=own,
            in_specs=[SMEM, SMEM, VMEM, VMEM, VMEM],
            out_specs=VMEM,
            scratch_shapes=[pltpu.VMEM((size, 128), jnp.float32), pltpu.VMEM((size, DEPTH), jnp.bfloat16)],
            compiler_params=limit,
        )(counts, neighbours, left, right, direction)
        if sweep < ITERS - 1:
            call = talk(functools.partial(update_kernel, n, scale), n, 1 + sweep, own.shape, (whole,) * 3)
            direction, residual, field = call(in_specs=[VMEM] * 4, out_specs=(VMEM,) * 3)(part, direction, residual, field)
        else:
            call = talk(
                functools.partial(finish_kernel, n, scale), n, 1 + sweep, (8, 128), (own,) * 2,
                [pltpu.VMEM((8, 128), jnp.float32)],
            )
            field, residual = call(in_specs=[VMEM] * 4, out_specs=(VMEM,) * 2)(part, direction, residual, field)
    return field.reshape(-1), residual.reshape(-1)


def solution(mesh):
    return jax.shard_map(
        on_device,
        mesh=mesh,
        in_specs=(P(("chain", "row"), None), P(None, ("chain", "row")), P(("chain", "row"))),
        out_specs=(P(("chain", "row")), P(("chain", "row"))),
        check_vma=False,
    )
```

```python
import functools

import jax
import jax.numpy as jnp
from jax import lax
from jax.experimental import pallas as pl
from jax.experimental.pallas import tpu as pltpu
from jax.sharding import PartitionSpec as P

ITERS = 3
DEPTH = 32
MESH = pl.DeviceIdType.MESH

nugget = 1.0
kernel_scale = 10.0

VMEM = pl.BlockSpec(memory_space=pltpu.VMEM)
SMEM = pl.BlockSpec(memory_space=pltpu.SMEM)


def exchange(n, block, landed, send, recv):
    me = lax.axis_index("row")
    barrier = pltpu.get_barrier_semaphore()

    def greet(i, carry):
        pl.semaphore_signal(barrier, inc=1, device_id={"row": lax.rem(me + i, n)}, device_id_type=MESH)
        return carry

    lax.fori_loop(1, n, greet, 0)
    pl.semaphore_wait(barrier, n - 1)

    def copy(i, place):
        return pltpu.make_async_remote_copy(
            src_ref=block,
            dst_ref=landed.at[place],
            send_sem=send.at[i],
            recv_sem=recv.at[i],
            device_id={"row": lax.rem(me + i, n)},
            device_id_type=MESH,
        )

    def begin(i, carry):
        copy(i, me).start()
        return carry

    def end(i, carry):
        copy(i, me).wait_send()
        copy(i, lax.rem(me - i + n, n)).wait_recv()
        return carry

    lax.fori_loop(1, n, begin, 0)
    landed[me] = block[...]
    lax.fori_loop(1, n, end, 0)


def total(values):
    values = values[0] if values.shape[0] == 1 else jnp.sum(values, axis=0)
    return jnp.sum(values, keepdims=True)


def gather_kernel(n, block, every, landed, send, recv):
    exchange(n, block, landed, send, recv)
    every[...] = landed[...]


def in_order(slots, landed, ordered):
    n, tiles_here, _ = landed.shape

    def move(device, carry):
        for t in range(tiles_here):
            slot = slots[device * tiles_here + t]
            ordered[device, t : t + 1, :] = landed[slot // tiles_here, pl.ds(slot % tiles_here, 1), :]
        return carry

    lax.fori_loop(0, n, move, 0)


def update_kernel(
    n, scale, slots, block, direction, residual, field, next_direction, next_residual, next_field, ordered, landed, send, recv
):
    exchange(n, block, landed, send, recv)
    in_order(slots, landed, ordered)
    old, rest = direction[...], residual[...]
    image = nugget * old + scale * ordered[...]
    norm_now = total(rest * rest)
    alpha = norm_now / total(old * image)
    next_field[...] = field[...] + alpha[None] * old
    rest = rest - alpha[None] * image
    next_residual[...] = rest
    next_direction[...] = rest + (total(rest * rest) / norm_now)[None] * old


def finish_kernel(n, scale, slots, block, direction, residual, field, own_field, own_residual, ordered, landed, send, recv):
    me = lax.axis_index("row")
    exchange(n, block, landed, send, recv)
    in_order(slots, landed, ordered)
    old, rest = direction[...], residual[...]
    image = nugget * old + scale * ordered[...]
    alpha = total(rest * rest) / total(old * image)
    own_field[...] = field[me] + alpha * direction[me]
    own_residual[...] = residual[me] - alpha * (nugget * direction[me] + scale * ordered[me])


def talk(kernel, n, ident, block, outs, extra=()):
    return functools.partial(
        pl.pallas_call,
        kernel,
        out_shape=outs,
        scratch_shapes=[
            *extra,
            pltpu.VMEM((n, *block), jnp.float32),
            pltpu.SemaphoreType.DMA((n,)),
            pltpu.SemaphoreType.DMA((n,)),
        ],
        compiler_params=pltpu.CompilerParams(
            collective_id=ident, has_side_effects=True, vmem_limit_bytes=40 * 1024 * 1024
        ),
    )


def split(values):
    def rounded(part):
        return part.astype(jnp.bfloat16).astype(jnp.float32)

    high = rounded(values)
    rest = values - high
    middle = rounded(rest)
    return high, middle, rest - middle


def features_kernel(tiles, every, left, right):
    n, _, tiles_here, size = every.shape
    left[...] = jnp.zeros_like(left)
    right[...] = jnp.zeros_like(right)
    one = jnp.ones((1, size), jnp.float32)

    def centred(device, t):
        return jnp.concatenate([every[device, c, pl.ds(t, 1), :] for c in range(2)], axis=0) - 4.0

    def parts(point):
        norm = jnp.sum(point * point, axis=0, keepdims=True)
        return split(point), split(norm)

    def write(device, carry):
        for t in range(tiles_here):
            (h, m, l), norm = parts(centred(device, t))
            tile = device * tiles_here + t
            for k, rows in enumerate((h, m, h, m, l, h)):
                right[tile, 2 * k : 2 * k + 2, :] = rows
            for k in range(3):
                right[tile, 12 + k : 13 + k, :] = one
                right[tile, 15 + k : 16 + k, :] = norm[k]
        return carry

    lax.fori_loop(0, n, write, 0)
    for t in range(tiles_here):
        (h, m, l), norm = parts(centred(tiles[t] // tiles_here, tiles[t] % tiles_here))
        for k, rows in enumerate((h, h, m, m, h, l)):
            left[t, 2 * k : 2 * k + 2, :] = -2.0 * rows
        for k in range(3):
            left[t, 12 + k : 13 + k, :] = norm[k]
            left[t, 15 + k : 16 + k, :] = one


def operate_kernel(counts, neighbours, left, right, values, image, summed, turned):
    tiles_here, _, size = left.shape
    rows = 128

    def one_row(t, carry):
        summed[...] = jnp.zeros_like(summed)
        turned[...] = left[t].T.astype(jnp.bfloat16)

        def advance(position, carry):
            u = neighbours[t, position]
            v = values[u // tiles_here, pl.ds(u % tiles_here, 1), :]
            columns = right[u].astype(jnp.bfloat16)
            for c in range(size // rows):
                here = pl.ds(c * rows, rows)
                square = jnp.dot(turned[here, :], columns, preferred_element_type=jnp.float32)
                square = jnp.maximum(square, 1e-20)
                shrink = jnp.maximum(1.0 - square * lax.rsqrt(square), 0.0)
                fourth = shrink * shrink
                fourth = fourth * fourth
                term = fourth * (1.25 - shrink) * v
                added = term[:, :128]
                for k in range(1, size // 128):
                    added = added + term[:, k * 128 : (k + 1) * 128]
                summed[here, :] += added
            return carry

        lax.fori_loop(0, counts[t], advance, 0)
        image[pl.ds(t, 1), :] = jnp.sum(summed[...].T, axis=0, keepdims=True)
        return carry

    lax.fori_loop(0, tiles_here, one_row, 0)


def share(lists, n, tiles_here):
    lengths = jnp.sum((lists >= 0).astype(jnp.int32), axis=1)
    number = jnp.arange(n * tiles_here, dtype=jnp.int32)
    ahead = lengths[None, :] > lengths[:, None]
    ahead = ahead | ((lengths[None, :] == lengths[:, None]) & (number[None, :] < number[:, None]))
    rank = jnp.sum(ahead.astype(jnp.int32), axis=1)
    lap, place = rank // n, rank % n
    slots = jnp.where(lap % 2 == 0, place, n - 1 - place) * tiles_here + lap
    wanted = lax.axis_index("row") * tiles_here + jnp.arange(tiles_here, dtype=jnp.int32)
    hit = slots[None, :] == wanted[:, None]
    tiles = jnp.sum(jnp.where(hit, number[None, :], 0), axis=1)
    counts = jnp.sum(jnp.where(hit, lengths[None, :], 0), axis=1)
    mine = jnp.sum(jnp.where(hit[:, :, None], lists[None], 0), axis=1)
    return slots, tiles, counts, mine


def on_device(neighbours, coordinates, right_side):
    n = lax.axis_size("row")
    tiles_here = neighbours.shape[0]
    size = right_side.shape[0] // tiles_here
    tile_count = n * tiles_here
    scale = 4.0 * kernel_scale / size
    f32 = lambda *shape: jax.ShapeDtypeStruct(shape, jnp.float32)
    whole, own = f32(n, tiles_here, size), f32(tiles_here, size)
    limit = pltpu.CompilerParams(vmem_limit_bytes=48 * 1024 * 1024)

    lists = neighbours.astype(jnp.float32)
    lists = jnp.pad(lists, ((0, 0), (0, size - lists.shape[1])), constant_values=-1.0)
    packed = jnp.concatenate([coordinates.reshape(-1), right_side, lists.reshape(-1)]).reshape(4, tiles_here, size)
    block = packed.shape
    every = talk(functools.partial(gather_kernel, n), n, 0, block, f32(n, *block))(in_specs=[VMEM], out_specs=VMEM)(packed)
    lists = every[:, 3, :, : neighbours.shape[1]].reshape(tile_count, -1).astype(jnp.int32)
    slots, tiles, counts, lists = share(lists, n, tiles_here)
    left, right = pl.pallas_call(
        features_kernel,
        out_shape=(f32(tiles_here, DEPTH, size), f32(tile_count, DEPTH, size)),
        in_specs=[SMEM, VMEM],
        out_specs=(VMEM, VMEM),
        compiler_params=limit,
    )(tiles, every)
    residual = direction = every[:, 2]
    field = jnp.zeros(whole.shape, jnp.float32)
    for sweep in range(ITERS):
        part = pl.pallas_call(
            operate_kernel,
            out_shape=own,
            in_specs=[SMEM, SMEM, VMEM, VMEM, VMEM],
            out_specs=VMEM,
            scratch_shapes=[pltpu.VMEM((size, 128), jnp.float32), pltpu.VMEM((size, DEPTH), jnp.bfloat16)],
            compiler_params=limit,
        )(counts, lists, left, right, direction)
        last = sweep == ITERS - 1
        kernel = functools.partial(finish_kernel if last else update_kernel, n, scale)
        outs = (own,) * 2 if last else (whole,) * 3
        call = talk(kernel, n, 1 + sweep, own.shape, outs, [pltpu.VMEM(whole.shape, jnp.float32)])
        outs = call(in_specs=[SMEM] + [VMEM] * 4, out_specs=(VMEM,) * len(outs))(slots, part, direction, residual, field)
        if last:
            field, residual = outs
        else:
            direction, residual, field = outs
    return field.reshape(-1), residual.reshape(-1)


def solution(mesh):
    return jax.shard_map(
        on_device,
        mesh=mesh,
        in_specs=(P(("chain", "row"), None), P(None, ("chain", "row")), P(("chain", "row"))),
        out_specs=(P(("chain", "row")), P(("chain", "row"))),
        check_vma=False,
    )
```
